32 devices in a mesh: section: 4 (over y, x), dp: 8 (over z, core).
Axes of the slice: x: 2, y: 2, z: 4, core: 2. Of those that a mesh axis runs over, the one named last changes fastest.
Arguments:
- d_out: bfloat16 [4, 384, 4096], P('section', 'dp'), may hold values from -6 to 6
- down_weight: bfloat16 [4, 11264, 4096], P('section', 'dp'), may hold values from -0.0546875 to 0.0546875
- gate_weight: bfloat16 [4, 11264, 4096], P('section', 'dp'), may hold values from -0.0546875 to 0.0546875
- up_weight: bfloat16 [4, 11264, 4096], P('section', 'dp'), may hold values from -0.0546875 to 0.0546875
- gate_pre: bfloat16 [4, 384, 11264], P('section', 'dp'), may hold values from -6 to 6
- up_val: bfloat16 [4, 384, 11264], P('section', 'dp'), may hold values from -6 to 6
- block_rows: int32 [4, 16], P('section'), may hold values from 0 to 87, as said below
- block_cols: int32 [4, 16], P('section'), may hold values from 0 to 31, as said below
- block_owner: int32 [4, 16], P('section'), may hold values from 0 to 7, as said below
Outputs:
- grad_input: bfloat16 [4, 384, 4096], P('section', 'dp')
- block_grads: bfloat16 [4, 24, 128, 128], P('section', 'dp')
The draws below stay inside these ranges and needn't reach their ends.
Inputs may be any that keep to these rules, and one draw needn't show every extreme that they name: `block_rows`: the 16 (row, column) pairs of a section are all different. `block_cols`: the 16 (row, column) pairs of a section are all different. `block_owner`: in each section no replica owns more than 3 blocks, and one owns exactly 3.
All inputs are finite; a program needn't handle non-finite values.
Results may differ from the reference program's by a relative error of at most 0.018.
Values may be sent and summed in bfloat16 or wider, within the bound.
No kernel may reach another device: no remote copies, remote signals or barrier semaphores. Data moves between devices by JAX's collectives and lax.ppermute only.
A program may use at most 128 MiB of HBM per device.

```python
import jax
import jax.numpy as jnp
from jax import lax

D = 4096
FF = 11264
TOK_DEV = 48
CAP = 3
TOKENS = 384
NB = 16
N_SECTION = 4
N_DP = 8


def chosen_blocks(key):
    keys = jax.random.split(key, N_SECTION)
    total_blocks = FF // 128 * (D // 128)

    def one_section(section_key):
        return jax.random.permutation(section_key, total_blocks)[:NB].astype(jnp.int32)
    return jax.vmap(one_section)(keys)


def draw_block_rows(key, part):
    picked = chosen_blocks(jax.random.fold_in(key, 11))
    return (picked // (D // 128)).astype(jnp.int32)


def draw_block_cols(key, part):
    picked = chosen_blocks(jax.random.fold_in(key, 11))
    return (picked % (D // 128)).astype(jnp.int32)


def draw_block_owner(key, part):
    keys = jax.random.split(jax.random.fold_in(key, 23), N_SECTION)

    def one_section(section_key):
        key_full, key_pop, key_noise, key_perm = jax.random.split(section_key, 4)
        slot_ids = jnp.arange(N_DP * CAP, dtype=jnp.int32)
        owner_of = slot_ids // CAP
        full_owner = jax.random.randint(key_full, (), 0, N_DP, dtype=jnp.int32)
        popular = jax.random.randint(key_pop, (N_DP,), 0, 4096, dtype=jnp.int32)
        noise = jax.random.randint(key_noise, (N_DP * CAP,), 0, 4096, dtype=jnp.int32)
        priority = noise + popular[owner_of] + jnp.where(owner_of == full_owner, 1 << 14, 0).astype(jnp.int32)
        scores = priority * 4096 + slot_ids
        _, taken = lax.top_k(scores, NB)
        owners = owner_of[taken]
        order = jax.random.permutation(key_perm, NB)
        return owners[order].astype(jnp.int32)
    return jax.vmap(one_section)(keys)


def level_of(stream_key, dims, shards, least, largest):
    def one(dim, blocks):
        heights = jax.random.uniform(jax.random.fold_in(jax.random.fold_in(stream_key, 6), dim), (blocks,), jnp.float32, least / len(shards), largest / len(shards))
        return jnp.repeat(jnp.exp(heights), dims[dim] // blocks).reshape((-1,) + (1,) * (len(dims) - dim - 1))

    level = one(*shards[0])
    for cut in shards[1:]:
        level = level * one(*cut)
    return level


def bell_draw(rng, dims, deviation, bound, cuts=(), held_as=jnp.bfloat16):
    entries = jax.random.normal(rng, dims, jnp.float32) * deviation
    if len(cuts) > 0:
        entries = level_of(rng, dims, cuts, -0.22, 0.18) * entries
    return jnp.clip(entries, min=-bound, max=bound).astype(held_as)


def setup_inputs(seed: int = 0) -> dict:
    seeds = jax.random.split(jax.random.key(seed), 10)
    d_out = bell_draw(seeds[0], (N_SECTION, TOKENS, D), 1.0, 6.0, ((0, 4), (1, 8)))
    down_weight = bell_draw(seeds[1], (N_SECTION, FF, D), FF ** -0.5, 0.0546875, ((0, 4), (1, 8)))
    gate_weight = bell_draw(seeds[2], (N_SECTION, FF, D), FF ** -0.5, 0.0546875, ((0, 4), (1, 8)))
    up_weight = bell_draw(seeds[3], (N_SECTION, FF, D), FF ** -0.5, 0.0546875, ((0, 4), (1, 8)))
    gate_pre = bell_draw(seeds[4], (N_SECTION, TOKENS, FF), 1.0, 6.0, ((0, 4), (1, 8)))
    up_val = bell_draw(seeds[5], (N_SECTION, TOKENS, FF), 1.0, 6.0, ((0, 4), (1, 8)))
    block_rows = draw_block_rows(jax.random.fold_in(seeds[9], 71), 0)
    block_cols = draw_block_cols(jax.random.fold_in(seeds[9], 71), 0)
    block_owner = draw_block_owner(jax.random.fold_in(seeds[9], 71), 0)
    return dict(d_out=d_out, down_weight=down_weight, gate_weight=gate_weight, up_weight=up_weight, gate_pre=gate_pre, up_val=up_val, block_rows=block_rows, block_cols=block_cols, block_owner=block_owner)


def gelu_pair(values):
    coeff = 0.7978845608
    cubic = values * values * values
    tangent = jnp.tanh(coeff * (values + 0.044715 * cubic))
    activated = 0.5 * values * (1.0 + tangent)
    slope = 0.5 * (1.0 + tangent) + 0.5 * values * (1.0 - tangent * tangent) * coeff * (1.0 + 3.0 * 0.044715 * values * values)
    return activated, slope


def owner_slots(owners):
    count_blocks = owners.shape[0]
    same = owners[:, None] == owners[None, :]
    index_list = jnp.arange(count_blocks, dtype=jnp.int32)
    earlier = index_list[None, :] < index_list[:, None]
    return jnp.sum((same & earlier).astype(jnp.int32), axis=1).astype(jnp.int32)


def reference(d_out, down_weight, gate_weight, up_weight, gate_pre, up_val, block_rows, block_cols, block_owner):
    inputs = []
    all_blocks = []
    group = FF // N_DP
    for section_id in range(N_SECTION):
        grad_rows = d_out[section_id]
        weight = down_weight[section_id]
        dhidden = lax.dot_general(grad_rows, weight, (((1,), (1,)), ((), ())), preferred_element_type=jnp.float32).astype(jnp.bfloat16)
        gate_val = gate_pre[section_id].astype(jnp.float32)
        up_vals = up_val[section_id].astype(jnp.float32)
        activated, slope = gelu_pair(gate_val)
        dh_wide = dhidden.astype(jnp.float32)
        local_gate = (dh_wide * up_vals * slope).astype(jnp.bfloat16)
        local_up = (dh_wide * activated).astype(jnp.bfloat16)
        w_gate = gate_weight[section_id]
        w_up = up_weight[section_id]

        def group_term(total, group_id):
            first = (group_id * group).astype(jnp.int32)
            g_part = lax.dynamic_slice_in_dim(local_gate, first, group, 1)
            u_part = lax.dynamic_slice_in_dim(local_up, first, group, 1)
            wg_part = lax.dynamic_slice_in_dim(w_gate, first, group, 0)
            wu_part = lax.dynamic_slice_in_dim(w_up, first, group, 0)
            term = jnp.dot(g_part, wg_part, preferred_element_type=jnp.float32) + jnp.dot(u_part, wu_part, preferred_element_type=jnp.float32)
            term = lax.optimization_barrier(term.astype(jnp.bfloat16))
            return total + term.astype(jnp.float32), None

        dx_total, _ = lax.scan(group_term, jnp.zeros((TOKENS, D), jnp.float32), jnp.arange(N_DP, dtype=jnp.int32))
        inputs.append(dx_total.astype(jnp.bfloat16))

        hidden = (activated * up_vals).astype(jnp.bfloat16)
        row_ids = block_rows[section_id]
        col_ids = block_cols[section_id]
        hidden_sel = jnp.take(hidden.reshape(TOKENS, FF // 128, 128), row_ids, axis=1)
        grad_sel = jnp.take(grad_rows.reshape(TOKENS, D // 128, 128), col_ids, axis=1)

        def replica(total, replica_id):
            first_row = (replica_id * TOK_DEV).astype(jnp.int32)
            h_part = lax.dynamic_slice_in_dim(hidden_sel, first_row, TOK_DEV, 0).astype(jnp.float32)
            g_part = lax.dynamic_slice_in_dim(grad_sel, first_row, TOK_DEV, 0).astype(jnp.float32)
            term = jnp.einsum("tnf,tnd->nfd", h_part, g_part).astype(jnp.bfloat16)
            term = lax.optimization_barrier(term)
            return total + term.astype(jnp.float32), None

        start_total = jnp.zeros((NB, 128, 128), jnp.float32)
        summed, _ = lax.scan(replica, start_total, jnp.arange(N_DP, dtype=jnp.int32))
        summed = summed * (1.0 / N_DP)
        owners = block_owner[section_id]
        positions = owners * CAP + owner_slots(owners)
        buffer = jnp.zeros((N_DP * CAP, 128, 128), jnp.float32).at[positions].set(summed)
        all_blocks.append(buffer.astype(jnp.bfloat16))
    zero_rows = jnp.zeros((TOKENS, D), jnp.bfloat16)
    grad_input = jnp.stack(inputs[1:] + [zero_rows])
    return grad_input, jnp.stack(all_blocks)
```

```python
import jax
import jax.numpy as jnp
from jax import lax
from jax.sharding import PartitionSpec as P

CAP = 3
LANES = 128


def gelu(values):
    coeff = 0.7978845608
    tangent = jnp.tanh(coeff * (values + 0.044715 * (values * values * values)))
    return 0.5 * values * (1.0 + tangent)


def gelu_slope(values):
    coeff = 0.7978845608
    square = values * values
    tangent = jnp.tanh(coeff * (values + 0.044715 * (square * values)))
    return 0.5 * (1.0 + tangent) + 0.5 * values * (1.0 - tangent * tangent) * coeff * (
        1.0 + 3.0 * 0.044715 * square
    )


def owner_table(owners, replicas):
    blocks = jnp.arange(owners.shape[0], dtype=jnp.int32)
    earlier = (owners[:, None] == owners[None, :]) & (blocks[None, :] < blocks[:, None])
    slots = jnp.sum(earlier.astype(jnp.int32), axis=1)
    places = jnp.arange(replicas * CAP, dtype=jnp.int32)
    hit = (owners * CAP + slots)[None, :] == places[:, None]
    chosen = jnp.sum(jnp.where(hit, blocks[None, :], 0), axis=1)
    return chosen.reshape(replicas, CAP), jnp.any(hit, axis=1).reshape(replicas, CAP)


def rotated(value, by):
    devices = lax.axis_size("dp")
    pairs = [(i, (i + 2 * by) % devices) for i in range(devices)]
    return lax.ppermute(value, "dp", pairs)


def swapped(value):
    return lax.ppermute(value, "dp", [(i, i ^ 1) for i in range(lax.axis_size("dp"))])


def relayed(value, by):
    devices, sections = lax.axis_size("dp"), lax.axis_size("section")
    pairs = [
        (s * devices + i, (s - 1) * devices + (i - 2 * by) % devices)
        for s in range(1, sections)
        for i in range(devices)
    ]
    return lax.ppermute(value, ("section", "dp"), pairs)


def shards(d_out, down_weight, gate_weight, up_weight, gate_pre, up_val, rows, cols, owner):
    mine = d_out[0]
    w_down, w_gate, w_up = down_weight[0], gate_weight[0], up_weight[0]
    gate, up = gate_pre[0], up_val[0]
    tokens, width = mine.shape
    units = w_down.shape[0]
    replicas = lax.axis_size("dp")
    chips = replicas // 2
    me = lax.axis_index("dp")
    chip, core = me // 2, me % 2

    same = [mine] + [rotated(mine, r) for r in range(1, chips)]
    other = [swapped(part) for part in same]
    grads = jnp.concatenate(same + other, axis=0)

    chosen, present = owner_table(owner[0], replicas)
    row_ids = jnp.take(rows[0], chosen.reshape(-1))
    col_ids = jnp.take(cols[0], chosen.reshape(-1)).reshape(replicas, CAP)

    def picked(values):
        tiles = values.reshape(tokens, values.shape[1] // LANES, LANES)
        return jnp.take(tiles, row_ids, axis=1).astype(jnp.float32)

    hidden = jnp.where(present.reshape(1, -1, 1), gelu(picked(gate)) * picked(up), 0.0)
    hidden = hidden.astype(jnp.bfloat16).reshape(tokens, replicas, CAP * LANES)

    def columns_of(values, replica):
        return lax.dynamic_slice_in_dim(values, replica * units, units, 1)

    def with_hidden(replica):
        extra = lax.dynamic_index_in_dim(hidden, replica, 1, keepdims=False)
        return jnp.concatenate([columns_of(gate, replica), extra], axis=1)

    def up_columns(replica):
        return columns_of(up, replica)

    def exchanged(part):
        given = jnp.stack([part(2 * ((chip + r) % chips) + 1 - core) for r in range(chips)])
        taken = swapped(given)
        pieces = []
        for r in range(chips):
            both = jnp.stack([part(2 * ((chip + r) % chips) + core), taken[r]])
            pieces.append(both if r == 0 else rotated(both, r))
        return jnp.stack(pieces, axis=1)

    gate_all = exchanged(with_hidden).reshape(replicas * tokens, -1)
    up_all = exchanged(up_columns).reshape(replicas * tokens, -1).astype(jnp.float32)
    hidden_all = gate_all[:, units:]
    gate_all = gate_all[:, :units].astype(jnp.float32)

    dhidden = lax.dot_general(
        grads, w_down, (((1,), (1,)), ((), ())), preferred_element_type=jnp.float32
    ).astype(jnp.bfloat16)
    wide = dhidden.astype(jnp.float32)
    local_up = (wide * gelu(gate_all)).astype(jnp.bfloat16)
    local_gate = (wide * up_all * gelu_slope(gate_all)).astype(jnp.bfloat16)

    halves = 2
    step = width // halves
    results = []
    for h in range(halves):
        part = slice(h * step, (h + 1) * step)
        term = jnp.dot(local_up, w_up[:, part], preferred_element_type=jnp.float32) + jnp.dot(
            local_gate, w_gate[:, part], preferred_element_type=jnp.float32
        )
        term = term.astype(jnp.bfloat16).reshape(2, chips, tokens, step)
        pair = (term[0].astype(jnp.float32) + swapped(term[1]).astype(jnp.float32)).astype(jnp.bfloat16)
        total = jnp.zeros((tokens, step), jnp.float32)
        for r in range(chips):
            total = total + relayed(pair[r], r).astype(jnp.float32)
        results.append(total.astype(jnp.bfloat16))
    grad_input = jnp.concatenate(results, axis=1)

    my_cols = lax.dynamic_index_in_dim(col_ids, me, 0, keepdims=False)
    sums = []
    for k in range(CAP):
        block = lax.dynamic_slice_in_dim(grads, my_cols[k] * LANES, LANES, 1)
        sums.append(
            lax.dot_general(
                hidden_all[:, k * LANES : (k + 1) * LANES],
                block,
                (((0,), (0,)), ((), ())),
                preferred_element_type=jnp.float32,
            )
        )
    block_grads = (jnp.stack(sums) * (1.0 / replicas)).astype(jnp.bfloat16)
    return (grad_input[None], block_grads[None])


def solution(mesh):
    return jax.shard_map(
        shards,
        mesh=mesh,
        in_specs=(P("section", "dp", None),) * 6 + (P("section", None),) * 3,
        out_specs=(P("section", "dp", None), P("section", "dp", None, None)),
        check_vma=False,
    )
```

```python
import functools

import jax
import jax.numpy as jnp
from jax import lax
from jax.experimental import pallas as pl
from jax.experimental.pallas import tpu as pltpu
from jax.sharding import PartitionSpec as P

CAP = 3
LANES = 128
VMEM = 40 * 1024 * 1024
COST = pl.CostEstimate(flops=0, bytes_accessed=0, transcendentals=0)


def gelu(values):
    coeff = 0.7978845608
    tangent = jnp.tanh(coeff * (values + 0.044715 * (values * values * values)))
    return 0.5 * values * (1.0 + tangent)


def gelu_pair(values):
    coeff = 0.7978845608
    square = values * values
    tangent = jnp.tanh(coeff * (values + 0.044715 * (square * values)))
    activated = 0.5 * values * (1.0 + tangent)
    slope = 0.5 * (1.0 + tangent) + 0.5 * values * (1.0 - tangent * tangent) * coeff * (
        1.0 + 3.0 * 0.044715 * square
    )
    return activated, slope


def rotated(value, by):
    devices = lax.axis_size("dp")
    pairs = [(i, (i + 2 * by) % devices) for i in range(devices)]
    return lax.ppermute(value, "dp", pairs)


def swapped(value):
    return lax.ppermute(value, "dp", [(i, i ^ 1) for i in range(lax.axis_size("dp"))])


def relayed(value, by):
    devices, sections = lax.axis_size("dp"), lax.axis_size("section")
    pairs = [
        (s * devices + i, (s - 1) * devices + (i - 2 * by) % devices)
        for s in range(1, sections)
        for i in range(devices)
    ]
    return lax.ppermute(value, ("section", "dp"), pairs)


def after(value, *earlier):
    return lax.optimization_barrier((value,) + earlier)[0]


def hidden_kernel(rows_ref, owner_ref, gate_ref, up_ref, out_ref, count_ref):
    out_ref[...] = jnp.zeros_like(out_ref)
    for replica in range(count_ref.shape[0]):
        count_ref[replica] = 0

    def block(i, carry):
        replica = owner_ref[i]
        slot = count_ref[replica]
        count_ref[replica] = slot + 1
        part = pl.ds(pl.multiple_of(rows_ref[i] * LANES, LANES), LANES)
        value = gelu(gate_ref[:, part].astype(jnp.float32)) * up_ref[:, part].astype(jnp.float32)
        place = pl.ds(pl.multiple_of((replica * CAP + slot) * LANES, LANES), LANES)
        out_ref[:, place] = value.astype(jnp.bfloat16)
        return carry

    lax.fori_loop(0, rows_ref.shape[0], block, 0)


def hidden_blocks(rows, owner, gate, up, replicas):
    tokens = gate.shape[0]
    return pl.pallas_call(
        hidden_kernel,
        in_specs=[pl.BlockSpec(memory_space=pltpu.SMEM)] * 2 + [pl.BlockSpec(memory_space=pltpu.VMEM)] * 2,
        out_specs=pl.BlockSpec(memory_space=pltpu.VMEM),
        out_shape=jax.ShapeDtypeStruct((tokens, replicas * CAP * LANES), jnp.bfloat16),
        scratch_shapes=[pltpu.SMEM((replicas,), jnp.int32)],
        compiler_params=pltpu.CompilerParams(vmem_limit_bytes=VMEM),
        cost_estimate=COST,
        name="hidden_blocks",
    )(rows, owner, gate, up)


def hidden_grad_kernel(*refs):
    grads, (w_ref, out_ref, sum_ref) = refs[:-3], refs[-3:]
    rows = grads[0].shape[0]
    step = pl.program_id(0)
    value = lax.dot_general(
        jnp.concatenate([ref[...] for ref in grads], axis=0),
        w_ref[...],
        (((1,), (1,)), ((), ())),
        preferred_element_type=jnp.float32,
    )

    @pl.when(step == 0)
    def _():
        sum_ref[...] = value

    @pl.when(step > 0)
    def _():
        sum_ref[...] += value

    @pl.when(step == pl.num_programs(0) - 1)
    def _():
        out_ref[...] = sum_ref[...].astype(jnp.bfloat16)


def hidden_grad(grads, weight):
    rows, width = grads[0].shape
    units = weight.shape[0]
    tile = 4 * LANES
    out = (len(grads) * rows, units)
    return pl.pallas_call(
        hidden_grad_kernel,
        grid=(width // tile,),
        in_specs=[pl.BlockSpec((rows, tile), lambda i: (0, i))] * len(grads)
        + [pl.BlockSpec((units, tile), lambda i: (0, i))],
        out_specs=pl.BlockSpec(out, lambda i: (0, 0)),
        out_shape=jax.ShapeDtypeStruct(out, jnp.bfloat16),
        scratch_shapes=[pltpu.VMEM(out, jnp.float32)],
        compiler_params=pltpu.CompilerParams(vmem_limit_bytes=VMEM),
        cost_estimate=COST,
        name="hidden_grad",
    )(*grads, weight)


def gradients_kernel(dh_ref, *refs):
    given, (lg_ref, lu_ref) = refs[:-2], refs[-2:]
    units = dh_ref.shape[1]
    rows = given[0].shape[1]
    skip = CAP * LANES
    padded = (given[0].shape[2] - skip) // 2
    for f in range(2):
        for p, ref in enumerate(given):
            part = slice((f * len(given) + p) * rows, (f * len(given) + p + 1) * rows)
            wide = dh_ref[part, :].astype(jnp.float32)
            gate = ref[f, :, skip : skip + units].astype(jnp.float32)
            up = ref[f, :, skip + padded : skip + padded + units].astype(jnp.float32)
            activated, slope = gelu_pair(gate)
            lg_ref[part, :] = (wide * up * slope).astype(jnp.bfloat16)
            lu_ref[part, :] = (wide * activated).astype(jnp.bfloat16)


def local_gradients(dhidden, given):
    out = jax.ShapeDtypeStruct(dhidden.shape, jnp.bfloat16)
    return pl.pallas_call(
        gradients_kernel,
        in_specs=[pl.BlockSpec(memory_space=pltpu.VMEM)] * (1 + len(given)),
        out_specs=[pl.BlockSpec(memory_space=pltpu.VMEM)] * 2,
        out_shape=[out, out],
        compiler_params=pltpu.CompilerParams(vmem_limit_bytes=VMEM),
        cost_estimate=COST,
        name="local_gradients",
    )(dhidden, *given)


def term_kernel(lg_ref, lu_ref, wg_ref, wu_ref, same_ref, other_ref):
    term = jnp.dot(lg_ref[...], wg_ref[...], preferred_element_type=jnp.float32)
    term += jnp.dot(lu_ref[...], wu_ref[...], preferred_element_type=jnp.float32)
    term = term.astype(jnp.bfloat16).reshape(2, *same_ref.shape)
    same_ref[...] = term[0]
    other_ref[...] = term[1]


def terms(local_gate, local_up, w_gate, w_up, chips, first, width):
    rows, units = local_gate.shape
    tile = 4 * LANES
    out = (chips, rows // (2 * chips))
    return pl.pallas_call(
        term_kernel,
        grid=(width // tile,),
        in_specs=[pl.BlockSpec((rows, units), lambda i: (0, 0))] * 2
        + [pl.BlockSpec((units, tile), lambda i: (0, i + first // tile))] * 2,
        out_specs=[pl.BlockSpec(out + (tile,), lambda i: (0, 0, i))] * 2,
        out_shape=[jax.ShapeDtypeStruct(out + (width,), jnp.bfloat16)] * 2,
        compiler_params=pltpu.CompilerParams(vmem_limit_bytes=VMEM),
        cost_estimate=COST,
        name="terms",
    )(local_gate, local_up, w_gate, w_up)


def block_kernel(scale, cols_ref, *refs):
    out_ref = refs[-1]
    refs = refs[:-1]
    grads, hidden = refs[: len(refs) * 2 // 3], refs[len(refs) * 2 // 3 :]
    left = jnp.concatenate([ref[f] for ref in hidden for f in range(2)], axis=0)
    right = jnp.concatenate([ref[...] for ref in grads], axis=0)
    value = lax.dot_general(left, right, (((0,), (0,)), ((), ())), preferred_element_type=jnp.float32)
    out_ref[0] = (value * scale).astype(jnp.bfloat16)


def block_sums(cols, grads, hidden, scale):
    rows = grads[0].shape[0]
    return pl.pallas_call(
        functools.partial(block_kernel, scale),
        grid_spec=pltpu.PrefetchScalarGridSpec(
            num_scalar_prefetch=1,
            grid=(CAP,),
            in_specs=[pl.BlockSpec((rows, LANES), lambda k, cols_ref: (0, cols_ref[k]))] * len(grads)
            + [pl.BlockSpec((2, rows, LANES), lambda k, cols_ref: (0, 0, k))] * len(hidden),
            out_specs=pl.BlockSpec((1, LANES, LANES), lambda k, cols_ref: (k, 0, 0)),
        ),
        out_shape=jax.ShapeDtypeStruct((CAP, LANES, LANES), jnp.bfloat16),
        compiler_params=pltpu.CompilerParams(vmem_limit_bytes=VMEM),
        cost_estimate=COST,
        name="block_sums",
    )(cols, *grads, *hidden)


def summed(*values):
    total = values[0].astype(jnp.float32)
    for value in values[1:]:
        total = total + value.astype(jnp.float32)
    return total.astype(jnp.bfloat16)


def own_columns(rows_owner, cols, me):
    blocks = jnp.arange(cols.shape[0], dtype=jnp.int32)
    own = rows_owner == me
    earlier = own[None, :] & (blocks[None, :] < blocks[:, None])
    slots = jnp.sum(earlier.astype(jnp.int32), axis=1)
    hit = own[None, :] & (slots[None, :] == jnp.arange(CAP, dtype=jnp.int32)[:, None])
    return jnp.sum(jnp.where(hit, cols[None, :], 0), axis=1)


def shards(d_out, down_weight, gate_weight, up_weight, gate_pre, up_val, rows, cols, owner):
    mine = d_out[0]
    w_down, w_gate, w_up = down_weight[0], gate_weight[0], up_weight[0]
    gate, up = gate_pre[0], up_val[0]
    tokens = mine.shape[0]
    units = w_down.shape[0]
    replicas = lax.axis_size("dp")
    chips = replicas // 2
    me = lax.axis_index("dp")
    chip, core = me // 2, me % 2

    same = [mine] + [None] * (chips - 1)
    same[1] = rotated(mine, 1)
    if chips > 2:
        same[chips - 1] = rotated(mine, -1)
    for r in range(2, chips - 1):
        same[r] = rotated(same[r - 1], 1)

    slots = hidden_blocks(rows[0], owner[0], gate, up, replicas)
    fill = jnp.zeros((tokens, -units % LANES), jnp.bfloat16)

    def held(replica):
        parts = [lax.dynamic_slice_in_dim(slots, replica * CAP * LANES, CAP * LANES, 1)]
        for values in (gate, up):
            parts += [lax.dynamic_slice_in_dim(values, replica * units, units, 1), fill]
        return jnp.concatenate(parts, axis=1)

    def ahead(r, other):
        return 2 * ((chip + r) % chips) + (1 - core if other else core)

    taken = swapped(jnp.stack([held(ahead(r, True)) for r in range(chips)]))
    order = [0] + list(range(chips - 2, 0, -1)) + ([chips - 1] if chips > 2 else [])
    sent = {r: jnp.stack([held(ahead(r, False)), taken[r]]) for r in order}
    given = {r: rotated(after(sent[r], same[1], same[chips - 1]), r) if r else sent[r] for r in order}

    other = {r: swapped(same[r]) for r in order}
    grads = [part[r] for part in (same, other) for r in order]
    dhidden = hidden_grad([after(grads[0], *sent.values())] + grads[1:], w_down)
    local_gate, local_up = local_gradients(dhidden, [given[r] for r in order])

    parts = 2
    width = mine.shape[1] // parts
    pieces, earlier = [], []
    for part in range(parts):
        last = part == parts - 1
        kept, passed = terms(local_gate, local_up, w_gate, w_up, chips, part * width, width)
        passed = swapped(after(passed, *earlier) if earlier else passed)
        sums = {r: summed(kept[i], passed[i]) for i, r in enumerate(order)}
        step = relayed if last else lambda value, by: rotated(value, -by)
        total, running = [relayed(sums[0], 0) if last else sums[0]], None
        if chips > 1:
            total.append(step(sums[chips - 1], chips - 1))
        earlier = total[1:]
        for r in range(chips - 2, 0, -1):
            value = sums[r] if running is None else summed(sums[r], running)
            if r == 1:
                total.append(step(value, 1))
            else:
                running = rotated(value, -1)
                if len(earlier) < 2:
                    earlier.append(running)
        pieces.append(summed(*total) if last else relayed(summed(*total), 0))
    grad_input = jnp.concatenate(pieces, axis=1)

    block_grads = block_sums(
        after(own_columns(owner[0], cols[0], me), *sums.values()),
        [part[r] for r in order for part in (same, other)],
        [given[r] for r in order],
        1.0 / replicas,
    )
    return (grad_input[None], block_grads[None])


def solution(mesh):
    return jax.shard_map(
        shards,
        mesh=mesh,
        in_specs=(P("section", "dp", None),) * 6 + (P("section", None),) * 3,
        out_specs=(P("section", "dp", None), P("section", "dp", None, None)),
        check_vma=False,
    )
```

```python
import functools

import jax
import jax.numpy as jnp
from jax import lax
from jax.experimental import pallas as pl
from jax.experimental.pallas import tpu as pltpu
from jax.sharding import PartitionSpec as P

CAP = 3
LANES = 128
VMEM = 40 * 1024 * 1024
COST = pl.CostEstimate(flops=0, bytes_accessed=0, transcendentals=0)


def gelu(values):
    coeff = 0.7978845608
    tangent = jnp.tanh(coeff * (values + 0.044715 * (values * values * values)))
    return 0.5 * values * (1.0 + tangent)


def gelu_pair(values):
    coeff = 0.7978845608
    square = values * values
    tangent = jnp.tanh(coeff * (values + 0.044715 * (square * values)))
    activated = 0.5 * values * (1.0 + tangent)
    slope = 0.5 * (1.0 + tangent) + 0.5 * values * (1.0 - tangent * tangent) * coeff * (
        1.0 + 3.0 * 0.044715 * square
    )
    return activated, slope


def rotated(value, by):
    devices = lax.axis_size("dp")
    pairs = [(i, (i + 2 * by) % devices) for i in range(devices)]
    return lax.ppermute(value, "dp", pairs)


def swapped(value):
    return lax.ppermute(value, "dp", [(i, i ^ 1) for i in range(lax.axis_size("dp"))])


def moved(value, routes):
    devices = lax.axis_size("dp")
    pairs = [
        (first * devices + i, last * devices + (i + 2 * by) % devices)
        for first, last, by in routes
        for i in range(devices)
    ]
    return lax.ppermute(value, ("section", "dp"), pairs)


def relayed(value, by):
    return moved(value, [(s, s - 1, -by) for s in range(1, lax.axis_size("section"))])


def after(value, *earlier):
    return lax.optimization_barrier((value,) + earlier)[0]


def hidden_kernel(rows_ref, owner_ref, gate_ref, up_ref, out_ref, count_ref):
    out_ref[...] = jnp.zeros_like(out_ref)
    for replica in range(count_ref.shape[0]):
        count_ref[replica] = 0

    def block(i, carry):
        replica = owner_ref[i]
        slot = count_ref[replica]
        count_ref[replica] = slot + 1
        part = pl.ds(pl.multiple_of(rows_ref[i] * LANES, LANES), LANES)
        value = gelu(gate_ref[:, part].astype(jnp.float32)) * up_ref[:, part].astype(jnp.float32)
        place = pl.ds(pl.multiple_of((replica * CAP + slot) * LANES, LANES), LANES)
        out_ref[:, place] = value.astype(jnp.bfloat16)
        return carry

    lax.fori_loop(0, rows_ref.shape[0], block, 0)


def hidden_blocks(rows, owner, gate, up, replicas):
    tokens = gate.shape[0]
    return pl.pallas_call(
        hidden_kernel,
        in_specs=[pl.BlockSpec(memory_space=pltpu.SMEM)] * 2 + [pl.BlockSpec(memory_space=pltpu.VMEM)] * 2,
        out_specs=pl.BlockSpec(memory_space=pltpu.VMEM),
        out_shape=jax.ShapeDtypeStruct((tokens, replicas * CAP * LANES), jnp.bfloat16),
        scratch_shapes=[pltpu.SMEM((replicas,), jnp.int32)],
        compiler_params=pltpu.CompilerParams(vmem_limit_bytes=VMEM),
        cost_estimate=COST,
        name="hidden_blocks",
    )(rows, owner, gate, up)


def hidden_grad_kernel(*refs):
    same, (other_ref, w_ref, out_ref, sum_ref) = refs[:-4], refs[-4:]
    step = pl.program_id(0)
    value = lax.dot_general(
        jnp.concatenate([ref[...] for ref in same] + [other_ref[p] for p in range(len(same))], axis=0),
        w_ref[...],
        (((1,), (1,)), ((), ())),
        preferred_element_type=jnp.float32,
    )

    @pl.when(step == 0)
    def _():
        sum_ref[...] = value

    @pl.when(step > 0)
    def _():
        sum_ref[...] += value

    @pl.when(step == pl.num_programs(0) - 1)
    def _():
        out_ref[...] = sum_ref[...].astype(jnp.bfloat16)


def hidden_grad(same, other, weight):
    rows, width = same[0].shape
    units = weight.shape[0]
    tile = 8 * LANES
    out = (2 * len(same) * rows, units)
    return pl.pallas_call(
        hidden_grad_kernel,
        grid=(width // tile,),
        in_specs=[pl.BlockSpec((rows, tile), lambda i: (0, i))] * len(same)
        + [pl.BlockSpec((len(same), rows, tile), lambda i: (0, 0, i)), pl.BlockSpec((units, tile), lambda i: (0, i))],
        out_specs=pl.BlockSpec(out, lambda i: (0, 0)),
        out_shape=jax.ShapeDtypeStruct(out, jnp.bfloat16),
        scratch_shapes=[pltpu.VMEM(out, jnp.float32)],
        compiler_params=pltpu.CompilerParams(vmem_limit_bytes=VMEM),
        cost_estimate=COST,
        name="hidden_grad",
    )(*same, other, weight)


def gradients_kernel(blocks, dh_ref, *refs):
    given, (lg_ref, lu_ref) = refs[:-2], refs[-2:]
    units = dh_ref.shape[1]
    rows = given[0].shape[1]
    padded = given[0].shape[2] // 2
    for b, (i, f) in enumerate(blocks):
        part = slice(b * rows, (b + 1) * rows)
        wide = dh_ref[part, :].astype(jnp.float32)
        gate = given[i][f, :, :units].astype(jnp.float32)
        up = given[i][f, :, padded : padded + units].astype(jnp.float32)
        activated, slope = gelu_pair(gate)
        lg_ref[part, :] = (wide * up * slope).astype(jnp.bfloat16)
        lu_ref[part, :] = (wide * activated).astype(jnp.bfloat16)


def local_gradients(dhidden, given, blocks):
    out = jax.ShapeDtypeStruct(dhidden.shape, jnp.bfloat16)
    return pl.pallas_call(
        functools.partial(gradients_kernel, blocks),
        in_specs=[pl.BlockSpec(memory_space=pltpu.VMEM)] * (1 + len(given)),
        out_specs=[pl.BlockSpec(memory_space=pltpu.VMEM)] * 2,
        out_shape=[out, out],
        compiler_params=pltpu.CompilerParams(vmem_limit_bytes=VMEM),
        cost_estimate=COST,
        name="local_gradients",
    )(dhidden, *given)


def term_kernel(lg_ref, lu_ref, wg_ref, wu_ref, same_ref, other_ref):
    term = jnp.dot(lg_ref[...], wg_ref[...], preferred_element_type=jnp.float32)
    term += jnp.dot(lu_ref[...], wu_ref[...], preferred_element_type=jnp.float32)
    term = term.astype(jnp.bfloat16).reshape(2, *same_ref.shape)
    same_ref[...] = term[0]
    other_ref[...] = term[1]


def terms(local_gate, local_up, w_gate, w_up, chips, first, width):
    rows, units = local_gate.shape
    tile = 4 * LANES
    out = (chips, rows // (2 * chips))
    return pl.pallas_call(
        term_kernel,
        grid=(width // tile,),
        in_specs=[pl.BlockSpec((rows, units), lambda i: (0, 0))] * 2
        + [pl.BlockSpec((units, tile), lambda i: (0, i + first // tile))] * 2,
        out_specs=[pl.BlockSpec(out + (tile,), lambda i: (0, 0, i))] * 2,
        out_shape=[jax.ShapeDtypeStruct(out + (width,), jnp.bfloat16)] * 2,
        compiler_params=pltpu.CompilerParams(vmem_limit_bytes=VMEM),
        cost_estimate=COST,
        name="terms",
    )(local_gate, local_up, w_gate, w_up)


def block_kernel(scale, cols_ref, other_ref, *refs):
    refs, out_ref = refs[:-1], refs[-1]
    same, hidden = refs[: len(refs) // 2], refs[len(refs) // 2 :]
    left = jnp.concatenate([ref[f] for f in range(2) for ref in hidden], axis=0)
    right = jnp.concatenate([ref[...] for ref in same] + [other_ref[p] for p in range(len(same))], axis=0)
    value = lax.dot_general(left, right, (((0,), (0,)), ((), ())), preferred_element_type=jnp.float32)
    out_ref[0] = (value * scale).astype(jnp.bfloat16)


def block_sums(cols, same, other, hidden, scale):
    rows = same[0].shape[0]
    return pl.pallas_call(
        functools.partial(block_kernel, scale),
        grid_spec=pltpu.PrefetchScalarGridSpec(
            num_scalar_prefetch=1,
            grid=(CAP,),
            in_specs=[pl.BlockSpec((len(same), rows, LANES), lambda k, cols_ref: (0, 0, cols_ref[k]))]
            + [pl.BlockSpec((rows, LANES), lambda k, cols_ref: (0, cols_ref[k]))] * len(same)
            + [pl.BlockSpec((2, rows, LANES), lambda k, cols_ref: (0, 0, k))] * len(hidden),
            out_specs=pl.BlockSpec((1, LANES, LANES), lambda k, cols_ref: (k, 0, 0)),
        ),
        out_shape=jax.ShapeDtypeStruct((CAP, LANES, LANES), jnp.bfloat16),
        compiler_params=pltpu.CompilerParams(vmem_limit_bytes=VMEM),
        cost_estimate=COST,
        name="block_sums",
    )(cols, other, *same, *hidden)


def summed(*values):
    total = values[0].astype(jnp.float32)
    for value in values[1:]:
        total = total + value.astype(jnp.float32)
    return total.astype(jnp.bfloat16)


def own_columns(rows_owner, cols, me):
    blocks = jnp.arange(cols.shape[0], dtype=jnp.int32)
    own = rows_owner == me
    earlier = own[None, :] & (blocks[None, :] < blocks[:, None])
    slots = jnp.sum(earlier.astype(jnp.int32), axis=1)
    hit = own[None, :] & (slots[None, :] == jnp.arange(CAP, dtype=jnp.int32)[:, None])
    return jnp.sum(jnp.where(hit, cols[None, :], 0), axis=1)


def shards(d_out, down_weight, gate_weight, up_weight, gate_pre, up_val, rows, cols, owner):
    mine = d_out[0]
    w_down, w_gate, w_up = down_weight[0], gate_weight[0], up_weight[0]
    gate, up = gate_pre[0], up_val[0]
    tokens = mine.shape[0]
    units = w_down.shape[0]
    replicas = lax.axis_size("dp")
    chips = replicas // 2
    me = lax.axis_index("dp")
    chip, core = me // 2, me % 2

    sections = lax.axis_size("section")
    section = lax.axis_index("section")

    same = [mine] + [None] * (chips - 1)
    same[1] = rotated(mine, 1)
    if chips > 2:
        same[chips - 1] = rotated(mine, -1)
    for r in range(chips - 2, 1, -1):
        same[r] = rotated(after(same[r + 1], same[1]) if r == chips - 2 else same[r + 1], -1)

    slots = hidden_blocks(rows[0], owner[0], gate, up, replicas)
    skip = CAP * LANES
    fill = jnp.zeros((tokens, -units % LANES), jnp.bfloat16)

    def held(replica):
        parts = [lax.dynamic_slice_in_dim(slots, replica * skip, skip, 1)]
        for values in (gate, up):
            parts += [lax.dynamic_slice_in_dim(values, replica * units, units, 1), fill]
        return jnp.concatenate(parts, axis=1)

    def ahead(r, other):
        return 2 * ((chip + r) % chips) + (1 - core if other else core)

    taken = swapped(jnp.stack([held(ahead(r, True)) for r in range(chips)]))
    both = [jnp.stack([held(ahead(r, False)), taken[r]]) for r in range(chips)]
    columns = [value[:, :, skip:] for value in both]

    far = chips // 2
    needed = range(1, sections)
    order = [0] + list(range(chips - 2, 0, -1)) + ([chips - 1] if chips > 2 else [])
    passing = {s: moved(columns[far][:1], [(s, 0, 0)]) for s in needed}
    sent, arrived = [], {0: columns[0]}
    for r in order[1:]:
        if r != far:
            sent.append(after(columns[r], same[1], same[chips - 1]))
            arrived[r] = moved(sent[-1], [(s, s, r) for s in needed])
    halves = [jnp.zeros_like(passing[s]) for s in range(1, 3)]
    for k in range(sections - 1):
        through, direct = 1 + k, 1 + (k + 1) % (sections - 1)
        value = jnp.where(section == 0, passing[through], columns[far][1:])
        sent.append(after(value, same[1], same[chips - 1]))
        value = moved(sent[-1], [(0, through, far), (direct, direct, far)])
        halves = [jnp.where(section == s, value, half) for s, half in zip((through, direct), halves)]
    given = [arrived[r] for r in order if r != far] + halves
    blocks = []
    for f in range(2):
        nth = iter(range(chips))
        blocks += [(chips - 1 + f, 0) if r == far else (next(nth), f) for r in order]

    other = swapped(jnp.stack([same[r] for r in order]))
    dhidden = hidden_grad([after(same[0], *sent)] + [same[r] for r in order[1:]], other, w_down)
    local_gate, local_up = local_gradients(dhidden, given, blocks)
    hidden = [both[0][:, :, :skip]]
    hidden += [rotated(after(both[r][:, :, :skip], dhidden), r) for r in order[1:]]

    parts = 1
    width = mine.shape[1] // parts
    pieces, earlier = [], hidden[1:]
    for part in range(parts):
        kept, passed = terms(local_gate, local_up, w_gate, w_up, chips, part * width, width)
        passed = swapped(after(passed, *earlier) if earlier else passed)
        sums = {r: summed(kept[i], passed[i]) for i, r in enumerate(order)}
        total, running = [relayed(sums[0], 0)], None
        if chips > 1:
            total.append(relayed(sums[chips - 1], chips - 1))
        earlier = total[:]
        for r in range(chips - 2, 0, -1):
            value = sums[r] if running is None else summed(sums[r], running)
            if r == 1:
                total.append(relayed(value, 1))
            else:
                running = rotated(value, -1)
                if len(earlier) < 3:
                    earlier.append(running)
        pieces.append(summed(*total))
    grad_input = jnp.concatenate(pieces, axis=1)

    block_grads = block_sums(
        after(own_columns(owner[0], cols[0], me), *sums.values()),
        [same[r] for r in order],
        other,
        hidden,
        1.0 / replicas,
    )
    return (grad_input[None], block_grads[None])


def solution(mesh):
    return jax.shard_map(
        shards,
        mesh=mesh,
        in_specs=(P("section", "dp", None),) * 6 + (P("section", None),) * 3,
        out_specs=(P("section", "dp", None), P("section", "dp", None, None)),
        check_vma=False,
    )
```

```python
import functools

import jax
import jax.numpy as jnp
from jax import lax
from jax.experimental import pallas as pl
from jax.experimental.pallas import tpu as pltpu
from jax.sharding import PartitionSpec as P

CAP = 3
LANES = 128
VMEM = 40 * 1024 * 1024
COST = pl.CostEstimate(flops=0, bytes_accessed=0, transcendentals=0)


def gelu(values):
    coeff = 0.7978845608
    tangent = jnp.tanh(coeff * (values + 0.044715 * (values * values * values)))
    return 0.5 * values * (1.0 + tangent)


def gelu_pair(values):
    coeff = 0.7978845608
    square = values * values
    tangent = jnp.tanh(coeff * (values + 0.044715 * (square * values)))
    activated = 0.5 * values * (1.0 + tangent)
    slope = 0.5 * (1.0 + tangent) + 0.5 * values * (1.0 - tangent * tangent) * coeff * (
        1.0 + 3.0 * 0.044715 * square
    )
    return activated, slope


def rotated(value, by):
    devices = lax.axis_size("dp")
    pairs = [(i, (i + 2 * by) % devices) for i in range(devices)]
    return lax.ppermute(value, "dp", pairs)


def swapped(value):
    return lax.ppermute(value, "dp", [(i, i ^ 1) for i in range(lax.axis_size("dp"))])


def moved(value, routes):
    devices = lax.axis_size("dp")
    pairs = [
        (first * devices + i, last * devices + (i + 2 * by) % devices)
        for first, last, by in routes
        for i in range(devices)
    ]
    return lax.ppermute(value, ("section", "dp"), pairs)


def relayed(value, by):
    return moved(value, [(s, s - 1, -by) for s in range(1, lax.axis_size("section"))])


def after(value, *earlier):
    return lax.optimization_barrier((value,) + earlier)[0]


def hidden_kernel(rows_ref, owner_ref, gate_ref, up_ref, out_ref, count_ref):
    out_ref[...] = jnp.zeros_like(out_ref)
    for replica in range(count_ref.shape[0]):
        count_ref[replica] = 0

    def block(i, carry):
        replica = owner_ref[i]
        slot = count_ref[replica]
        count_ref[replica] = slot + 1
        part = pl.ds(pl.multiple_of(rows_ref[i] * LANES, LANES), LANES)
        value = gelu(gate_ref[:, part].astype(jnp.float32)) * up_ref[:, part].astype(jnp.float32)
        place = pl.ds(pl.multiple_of((replica * CAP + slot) * LANES, LANES), LANES)
        out_ref[:, place] = value.astype(jnp.bfloat16)
        return carry

    lax.fori_loop(0, rows_ref.shape[0], block, 0)


def hidden_blocks(rows, owner, gate, up, replicas):
    tokens = gate.shape[0]
    return pl.pallas_call(
        hidden_kernel,
        in_specs=[pl.BlockSpec(memory_space=pltpu.SMEM)] * 2 + [pl.BlockSpec(memory_space=pltpu.VMEM)] * 2,
        out_specs=pl.BlockSpec(memory_space=pltpu.VMEM),
        out_shape=jax.ShapeDtypeStruct((tokens, replicas * CAP * LANES), jnp.bfloat16),
        scratch_shapes=[pltpu.SMEM((replicas,), jnp.int32)],
        compiler_params=pltpu.CompilerParams(vmem_limit_bytes=VMEM),
        cost_estimate=COST,
        name="hidden_blocks",
    )(rows, owner, gate, up)


def hidden_grad_kernel(*refs):
    same, (other_ref, w_ref, out_ref, sum_ref) = refs[:-4], refs[-4:]
    step = pl.program_id(0)
    value = lax.dot_general(
        jnp.concatenate([ref[...] for ref in same] + [other_ref[p] for p in range(len(same))], axis=0),
        w_ref[...],
        (((1,), (1,)), ((), ())),
        preferred_element_type=jnp.float32,
    )

    @pl.when(step == 0)
    def _():
        sum_ref[...] = value

    @pl.when(step > 0)
    def _():
        sum_ref[...] += value

    @pl.when(step == pl.num_programs(0) - 1)
    def _():
        out_ref[...] = sum_ref[...].astype(jnp.bfloat16)


def hidden_grad(same, other, weight):
    rows, width = same[0].shape
    units = weight.shape[0]
    tile = 8 * LANES
    out = (2 * len(same) * rows, units)
    return pl.pallas_call(
        hidden_grad_kernel,
        grid=(width // tile,),
        in_specs=[pl.BlockSpec((rows, tile), lambda i: (0, i))] * len(same)
        + [pl.BlockSpec((len(same), rows, tile), lambda i: (0, 0, i)), pl.BlockSpec((units, tile), lambda i: (0, i))],
        out_specs=pl.BlockSpec(out, lambda i: (0, 0)),
        out_shape=jax.ShapeDtypeStruct(out, jnp.bfloat16),
        scratch_shapes=[pltpu.VMEM(out, jnp.float32)],
        compiler_params=pltpu.CompilerParams(vmem_limit_bytes=VMEM),
        cost_estimate=COST,
        name="hidden_grad",
    )(*same, other, weight)


def gradients_kernel(blocks, dh_ref, *refs):
    given, out_ref = refs[:-1], refs[-1]
    units = dh_ref.shape[1]
    rows = given[0].shape[1]
    padded = given[0].shape[2] // 2
    for b, (i, f) in enumerate(blocks):
        part = slice(b * rows, (b + 1) * rows)
        wide = dh_ref[part, :].astype(jnp.float32)
        gate = given[i][f, :, :units].astype(jnp.float32)
        up = given[i][f, :, padded : padded + units].astype(jnp.float32)
        activated, slope = gelu_pair(gate)
        out_ref[part, :units] = (wide * up * slope).astype(jnp.bfloat16)
        out_ref[part, units:] = (wide * activated).astype(jnp.bfloat16)


def local_gradients(dhidden, given, blocks):
    rows, units = dhidden.shape
    return pl.pallas_call(
        functools.partial(gradients_kernel, blocks),
        in_specs=[pl.BlockSpec(memory_space=pltpu.VMEM)] * (1 + len(given)),
        out_specs=pl.BlockSpec(memory_space=pltpu.VMEM),
        out_shape=jax.ShapeDtypeStruct((rows, 2 * units), jnp.bfloat16),
        compiler_params=pltpu.CompilerParams(vmem_limit_bytes=VMEM),
        cost_estimate=COST,
        name="local_gradients",
    )(dhidden, *given)


def term_kernel(local_ref, wg_ref, wu_ref, same_ref, other_ref):
    weight = jnp.concatenate([wg_ref[...], wu_ref[...]], axis=0)
    term = jnp.dot(local_ref[...], weight, preferred_element_type=jnp.float32)
    term = term.astype(jnp.bfloat16).reshape(2, *same_ref.shape)
    same_ref[...] = term[0]
    other_ref[...] = term[1]


def terms(local, w_gate, w_up, chips, first, width):
    rows, units = local.shape[0], w_gate.shape[0]
    tile = 8 * LANES
    out = (chips, rows // (2 * chips))
    return pl.pallas_call(
        term_kernel,
        grid=(width // tile,),
        in_specs=[pl.BlockSpec((rows, 2 * units), lambda i: (0, 0))]
        + [pl.BlockSpec((units, tile), lambda i: (0, i + first // tile))] * 2,
        out_specs=[pl.BlockSpec(out + (tile,), lambda i: (0, 0, i))] * 2,
        out_shape=[jax.ShapeDtypeStruct(out + (width,), jnp.bfloat16)] * 2,
        compiler_params=pltpu.CompilerParams(vmem_limit_bytes=VMEM),
        cost_estimate=COST,
        name="terms",
    )(local, w_gate, w_up)


def block_kernel(scale, cols_ref, other_ref, *refs):
    refs, out_ref = refs[:-1], refs[-1]
    same, hidden = refs[: len(refs) // 2], refs[len(refs) // 2 :]
    left = jnp.concatenate([ref[f] for f in range(2) for ref in hidden], axis=0)
    right = jnp.concatenate([ref[...] for ref in same] + [other_ref[p] for p in range(len(same))], axis=0)
    value = lax.dot_general(left, right, (((0,), (0,)), ((), ())), preferred_element_type=jnp.float32)
    out_ref[0] = (value * scale).astype(jnp.bfloat16)


def block_sums(cols, same, other, hidden, scale):
    rows = same[0].shape[0]
    return pl.pallas_call(
        functools.partial(block_kernel, scale),
        grid_spec=pltpu.PrefetchScalarGridSpec(
            num_scalar_prefetch=1,
            grid=(CAP,),
            in_specs=[pl.BlockSpec((len(same), rows, LANES), lambda k, cols_ref: (0, 0, cols_ref[k]))]
            + [pl.BlockSpec((rows, LANES), lambda k, cols_ref: (0, cols_ref[k]))] * len(same)
            + [pl.BlockSpec((2, rows, LANES), lambda k, cols_ref: (0, 0, k))] * len(hidden),
            out_specs=pl.BlockSpec((1, LANES, LANES), lambda k, cols_ref: (k, 0, 0)),
        ),
        out_shape=jax.ShapeDtypeStruct((CAP, LANES, LANES), jnp.bfloat16),
        compiler_params=pltpu.CompilerParams(vmem_limit_bytes=VMEM),
        cost_estimate=COST,
        name="block_sums",
    )(cols, other, *same, *hidden)


def summed(*values):
    total = values[0].astype(jnp.float32)
    for value in values[1:]:
        total = total + value.astype(jnp.float32)
    return total.astype(jnp.bfloat16)


def own_columns(rows_owner, cols, me):
    blocks = jnp.arange(cols.shape[0], dtype=jnp.int32)
    own = rows_owner == me
    earlier = own[None, :] & (blocks[None, :] < blocks[:, None])
    slots = jnp.sum(earlier.astype(jnp.int32), axis=1)
    hit = own[None, :] & (slots[None, :] == jnp.arange(CAP, dtype=jnp.int32)[:, None])
    return jnp.sum(jnp.where(hit, cols[None, :], 0), axis=1)


def shards(d_out, down_weight, gate_weight, up_weight, gate_pre, up_val, rows, cols, owner):
    mine = d_out[0]
    w_down, w_gate, w_up = down_weight[0], gate_weight[0], up_weight[0]
    gate, up = gate_pre[0], up_val[0]
    tokens = mine.shape[0]
    units = w_down.shape[0]
    replicas = lax.axis_size("dp")
    chips = replicas // 2
    me = lax.axis_index("dp")
    chip, core = me // 2, me % 2

    sections = lax.axis_size("section")
    section = lax.axis_index("section")

    same = [mine] + [None] * (chips - 1)
    same[1] = rotated(mine, 1)
    if chips > 2:
        same[chips - 1] = rotated(mine, -1)
    for r in range(chips - 2, 1, -1):
        same[r] = rotated(same[r + 1], -1)

    slots = hidden_blocks(rows[0], owner[0], gate, up, replicas)
    skip = CAP * LANES
    fill = jnp.zeros((tokens, -units % LANES), jnp.bfloat16)

    def held(replica):
        parts = [lax.dynamic_slice_in_dim(slots, replica * skip, skip, 1)]
        for values in (gate, up):
            parts += [lax.dynamic_slice_in_dim(values, replica * units, units, 1), fill]
        return jnp.concatenate(parts, axis=1)

    def ahead(r, other):
        return 2 * ((chip + r) % chips) + (1 - core if other else core)

    taken = swapped(jnp.stack([held(ahead(r, True)) for r in range(chips)]))
    both = [jnp.stack([held(ahead(r, False)), taken[r]]) for r in range(chips)]
    columns = [value[:, :, skip:] for value in both]

    far = chips // 2
    needed = range(1, sections)
    order = [0] + list(range(chips - 2, 0, -1)) + ([chips - 1] if chips > 2 else [])
    passing = {s: moved(columns[far][:1], [(s, 0, 0)]) for s in needed}
    sent, arrived = [], {0: columns[0]}
    for r in order[1:]:
        if r != far:
            sent.append(after(columns[r], same[1], same[chips - 1]))
            arrived[r] = moved(sent[-1], [(s, s, r) for s in needed])
    halves = [jnp.zeros_like(passing[s]) for s in range(1, 3)]
    for k in range(sections - 1):
        through, direct = 1 + k, 1 + (k + 1) % (sections - 1)
        value = jnp.where(section == 0, passing[through], columns[far][1:])
        sent.append(after(value, same[1], same[chips - 1]))
        value = moved(sent[-1], [(0, through, far), (direct, direct, far)])
        halves = [jnp.where(section == s, value, half) for s, half in zip((through, direct), halves)]
    given = [arrived[r] for r in order if r != far] + halves
    blocks = []
    for f in range(2):
        nth = iter(range(chips))
        blocks += [(chips - 1 + f, 0) if r == far else (next(nth), f) for r in order]

    other = swapped(jnp.stack([same[r] for r in order]))
    dhidden = hidden_grad([after(same[0], *sent)] + [same[r] for r in order[1:]], other, w_down)
    local = local_gradients(dhidden, given, blocks)
    hidden = [both[0][:, :, :skip]]
    hidden += [rotated(after(both[r][:, :, :skip], dhidden), r) for r in order[1:]]

    parts = 1
    width = mine.shape[1] // parts
    pieces, earlier = [], hidden[1:]
    for part in range(parts):
        kept, passed = terms(local, w_gate, w_up, chips, part * width, width)
        passed = swapped(after(passed, *earlier) if earlier else passed)
        sums = {r: summed(kept[i], passed[i]) for i, r in enumerate(order)}
        total, running = [relayed(sums[0], 0)], None
        if chips > 1:
            total.append(relayed(sums[chips - 1], chips - 1))
        earlier = total[:]
        for r in range(chips - 2, 0, -1):
            value = sums[r] if running is None else summed(sums[r], running)
            if r == 1:
                total.append(relayed(value, 1))
            else:
                running = rotated(value, -1)
                if len(earlier) < 3:
                    earlier.append(running)
        pieces.append(summed(*total))
    grad_input = jnp.concatenate(pieces, axis=1)

    block_grads = block_sums(
        after(own_columns(owner[0], cols[0], me), *sums.values()),
        [same[r] for r in order],
        other,
        hidden,
        1.0 / replicas,
    )
    return (grad_input[None], block_grads[None])


def solution(mesh):
    return jax.shard_map(
        shards,
        mesh=mesh,
        in_specs=(P("section", "dp", None),) * 6 + (P("section", None),) * 3,
        out_specs=(P("section", "dp", None), P("section", "dp", None, None)),
        check_vma=False,
    )
```

```python
import functools

import jax
import jax.numpy as jnp
from jax import lax
from jax.experimental import pallas as pl
from jax.experimental.pallas import tpu as pltpu
from jax.sharding import PartitionSpec as P

CAP = 3
LANES = 128
VMEM = 40 * 1024 * 1024
COST = pl.CostEstimate(flops=0, bytes_accessed=0, transcendentals=0)


def gelu(values):
    coeff = 0.7978845608
    tangent = jnp.tanh(coeff * (values + 0.044715 * (values * values * values)))
    return 0.5 * values * (1.0 + tangent)


def gelu_pair(values):
    coeff = 0.7978845608
    square = values * values
    tangent = jnp.tanh(coeff * (values + 0.044715 * (square * values)))
    activated = 0.5 * values * (1.0 + tangent)
    slope = 0.5 * (1.0 + tangent) + 0.5 * values * (1.0 - tangent * tangent) * coeff * (
        1.0 + 3.0 * 0.044715 * square
    )
    return activated, slope


def rotated(value, by):
    devices = lax.axis_size("dp")
    pairs = [(i, (i + 2 * by) % devices) for i in range(devices)]
    return lax.ppermute(value, "dp", pairs)


def swapped(value):
    return lax.ppermute(value, "dp", [(i, i ^ 1) for i in range(lax.axis_size("dp"))])


def moved(value, routes):
    devices = lax.axis_size("dp")
    pairs = [
        (first * devices + i, last * devices + (i + 2 * by) % devices)
        for first, last, by in routes
        for i in range(devices)
    ]
    return lax.ppermute(value, ("section", "dp"), pairs)


def relayed(value, by):
    return moved(value, [(s, s - 1, -by) for s in range(1, lax.axis_size("section"))])


def after(value, *earlier):
    return lax.optimization_barrier((value,) + earlier)[0]


def hidden_kernel(rows_ref, owner_ref, gate_ref, up_ref, out_ref, count_ref):
    out_ref[...] = jnp.zeros_like(out_ref)
    for replica in range(count_ref.shape[0]):
        count_ref[replica] = 0

    def block(i, carry):
        replica = owner_ref[i]
        slot = count_ref[replica]
        count_ref[replica] = slot + 1
        part = pl.ds(pl.multiple_of(rows_ref[i] * LANES, LANES), LANES)
        value = gelu(gate_ref[:, part].astype(jnp.float32)) * up_ref[:, part].astype(jnp.float32)
        place = pl.ds(pl.multiple_of((replica * CAP + slot) * LANES, LANES), LANES)
        out_ref[:, place] = value.astype(jnp.bfloat16)
        return carry

    lax.fori_loop(0, rows_ref.shape[0], block, 0)


def hidden_blocks(rows, owner, gate, up, replicas):
    tokens = gate.shape[0]
    return pl.pallas_call(
        hidden_kernel,
        in_specs=[pl.BlockSpec(memory_space=pltpu.SMEM)] * 2 + [pl.BlockSpec(memory_space=pltpu.VMEM)] * 2,
        out_specs=pl.BlockSpec(memory_space=pltpu.VMEM),
        out_shape=jax.ShapeDtypeStruct((tokens, replicas * CAP * LANES), jnp.bfloat16),
        scratch_shapes=[pltpu.SMEM((replicas,), jnp.int32)],
        compiler_params=pltpu.CompilerParams(vmem_limit_bytes=VMEM),
        cost_estimate=COST,
        name="hidden_blocks",
    )(rows, owner, gate, up)


def hidden_grad_kernel(*refs):
    same, (other_ref, w_ref, out_ref, sum_ref) = refs[:-4], refs[-4:]
    step = pl.program_id(0)
    value = lax.dot_general(
        jnp.concatenate([ref[...] for ref in same] + [other_ref[p] for p in range(len(same))], axis=0),
        w_ref[...],
        (((1,), (1,)), ((), ())),
        preferred_element_type=jnp.float32,
    )

    @pl.when(step == 0)
    def _():
        sum_ref[...] = value

    @pl.when(step > 0)
    def _():
        sum_ref[...] += value

    @pl.when(step == pl.num_programs(0) - 1)
    def _():
        out_ref[...] = sum_ref[...].astype(jnp.bfloat16)


def hidden_grad(same, other, weight):
    rows, width = same[0].shape
    units = weight.shape[0]
    tile = 8 * LANES
    out = (2 * len(same) * rows, units)
    return pl.pallas_call(
        hidden_grad_kernel,
        grid=(width // tile,),
        in_specs=[pl.BlockSpec((rows, tile), lambda i: (0, i))] * len(same)
        + [pl.BlockSpec((len(same), rows, tile), lambda i: (0, 0, i)), pl.BlockSpec((units, tile), lambda i: (0, i))],
        out_specs=pl.BlockSpec(out, lambda i: (0, 0)),
        out_shape=jax.ShapeDtypeStruct(out, jnp.bfloat16),
        scratch_shapes=[pltpu.VMEM(out, jnp.float32)],
        compiler_params=pltpu.CompilerParams(vmem_limit_bytes=VMEM),
        cost_estimate=COST,
        name="hidden_grad",
    )(*same, other, weight)


def gradients_kernel(blocks, dh_ref, *refs):
    given, out_ref = refs[:-1], refs[-1]
    units = dh_ref.shape[1]
    rows = given[0].shape[1]
    padded = given[0].shape[2] // 2
    for b, (block, i, f) in enumerate(blocks):
        part = slice(b * rows, (b + 1) * rows)
        wide = dh_ref[block * rows : (block + 1) * rows, :].astype(jnp.float32)
        gate = given[i][f, :, :units].astype(jnp.float32)
        up = given[i][f, :, padded : padded + units].astype(jnp.float32)
        activated, slope = gelu_pair(gate)
        out_ref[part, :units] = (wide * up * slope).astype(jnp.bfloat16)
        out_ref[part, units:] = (wide * activated).astype(jnp.bfloat16)


def local_gradients(dhidden, given, blocks):
    rows, units = len(blocks) * given[0].shape[1], dhidden.shape[1]
    return pl.pallas_call(
        functools.partial(gradients_kernel, blocks),
        in_specs=[pl.BlockSpec(memory_space=pltpu.VMEM)] * (1 + len(given)),
        out_specs=pl.BlockSpec(memory_space=pltpu.VMEM),
        out_shape=jax.ShapeDtypeStruct((rows, 2 * units), jnp.bfloat16),
        compiler_params=pltpu.CompilerParams(vmem_limit_bytes=VMEM),
        cost_estimate=COST,
        name="local_gradients",
    )(dhidden, *given)


def term_kernel(near_ref, far_ref, wg_ref, wu_ref, same_ref, other_ref):
    weight = jnp.concatenate([wg_ref[...], wu_ref[...]], axis=0)
    local = jnp.concatenate([near_ref[...], far_ref[...]], axis=0)
    term = jnp.dot(local, weight, preferred_element_type=jnp.float32).astype(jnp.bfloat16)
    chips, rows, tile = same_ref.shape
    near = near_ref.shape[0]
    for f, ref in enumerate((same_ref, other_ref)):
        ref[: chips - 1] = term[f * near // 2 : (f + 1) * near // 2].reshape(chips - 1, rows, tile)
        ref[chips - 1] = term[near + f * rows : near + (f + 1) * rows]


def terms(near, far, w_gate, w_up, chips, first, width):
    units = w_gate.shape[0]
    tile = 8 * LANES
    out = (chips, far.shape[0] // 2)
    return pl.pallas_call(
        term_kernel,
        grid=(width // tile,),
        in_specs=[pl.BlockSpec(near.shape, lambda i: (0, 0)), pl.BlockSpec(far.shape, lambda i: (0, 0))]
        + [pl.BlockSpec((units, tile), lambda i: (0, i + first // tile))] * 2,
        out_specs=[pl.BlockSpec(out + (tile,), lambda i: (0, 0, i))] * 2,
        out_shape=[jax.ShapeDtypeStruct(out + (width,), jnp.bfloat16)] * 2,
        compiler_params=pltpu.CompilerParams(vmem_limit_bytes=VMEM),
        cost_estimate=COST,
        name="terms",
    )(near, far, w_gate, w_up)


def block_kernel(scale, cols_ref, other_ref, *refs):
    refs, out_ref = refs[:-1], refs[-1]
    same, hidden = refs[: len(refs) // 2], refs[len(refs) // 2 :]
    left = jnp.concatenate([ref[f] for f in range(2) for ref in hidden], axis=0)
    right = jnp.concatenate([ref[...] for ref in same] + [other_ref[p] for p in range(len(same))], axis=0)
    value = lax.dot_general(left, right, (((0,), (0,)), ((), ())), preferred_element_type=jnp.float32)
    out_ref[0] = (value * scale).astype(jnp.bfloat16)


def block_sums(cols, same, other, hidden, scale):
    rows = same[0].shape[0]
    return pl.pallas_call(
        functools.partial(block_kernel, scale),
        grid_spec=pltpu.PrefetchScalarGridSpec(
            num_scalar_prefetch=1,
            grid=(CAP,),
            in_specs=[pl.BlockSpec((len(same), rows, LANES), lambda k, cols_ref: (0, 0, cols_ref[k]))]
            + [pl.BlockSpec((rows, LANES), lambda k, cols_ref: (0, cols_ref[k]))] * len(same)
            + [pl.BlockSpec((2, rows, LANES), lambda k, cols_ref: (0, 0, k))] * len(hidden),
            out_specs=pl.BlockSpec((1, LANES, LANES), lambda k, cols_ref: (k, 0, 0)),
        ),
        out_shape=jax.ShapeDtypeStruct((CAP, LANES, LANES), jnp.bfloat16),
        compiler_params=pltpu.CompilerParams(vmem_limit_bytes=VMEM),
        cost_estimate=COST,
        name="block_sums",
    )(cols, other, *same, *hidden)


def summed(*values):
    total = values[0].astype(jnp.float32)
    for value in values[1:]:
        total = total + value.astype(jnp.float32)
    return total.astype(jnp.bfloat16)


def own_columns(rows_owner, cols, me):
    blocks = jnp.arange(cols.shape[0], dtype=jnp.int32)
    own = rows_owner == me
    earlier = own[None, :] & (blocks[None, :] < blocks[:, None])
    slots = jnp.sum(earlier.astype(jnp.int32), axis=1)
    hit = own[None, :] & (slots[None, :] == jnp.arange(CAP, dtype=jnp.int32)[:, None])
    return jnp.sum(jnp.where(hit, cols[None, :], 0), axis=1)


def shards(d_out, down_weight, gate_weight, up_weight, gate_pre, up_val, rows, cols, owner):
    mine = d_out[0]
    w_down, w_gate, w_up = down_weight[0], gate_weight[0], up_weight[0]
    gate, up = gate_pre[0], up_val[0]
    tokens = mine.shape[0]
    units = w_down.shape[0]
    replicas = lax.axis_size("dp")
    chips = replicas // 2
    me = lax.axis_index("dp")
    chip, core = me // 2, me % 2

    sections = lax.axis_size("section")
    section = lax.axis_index("section")

    same = [mine] + [None] * (chips - 1)
    same[1] = rotated(mine, 1)
    if chips > 2:
        same[chips - 1] = rotated(mine, -1)
    for r in range(chips - 2, 1, -1):
        same[r] = rotated(same[r + 1], -1)

    slots = hidden_blocks(rows[0], owner[0], gate, up, replicas)
    skip = CAP * LANES
    fill = jnp.zeros((tokens, -units % LANES), jnp.bfloat16)

    def held(replica):
        parts = [lax.dynamic_slice_in_dim(slots, replica * skip, skip, 1)]
        for values in (gate, up):
            parts += [lax.dynamic_slice_in_dim(values, replica * units, units, 1), fill]
        return jnp.concatenate(parts, axis=1)

    def ahead(r, other):
        return 2 * ((chip + r) % chips) + (1 - core if other else core)

    taken = swapped(jnp.stack([held(ahead(r, True)) for r in range(chips)]))
    both = [jnp.stack([held(ahead(r, False)), taken[r]]) for r in range(chips)]
    columns = [value[:, :, skip:] for value in both]

    far = chips // 2
    needed = range(1, sections)
    order = [r for r in range(chips) if r != far] + [far]
    passing = {s: moved(columns[far][:1], [(s, 0, 0)]) for s in needed}
    sent, arrived = [], {0: columns[0]}
    for r in order[1:]:
        if r != far:
            sent.append(after(columns[r], same[1], same[chips - 1]))
            arrived[r] = moved(sent[-1], [(s, s, r) for s in needed])
    halves = [jnp.zeros_like(passing[s]) for s in range(1, 3)]
    for k in range(sections - 1):
        through, direct = 1 + k, 1 + (k + 1) % (sections - 1)
        value = jnp.where(section == 0, passing[through], columns[far][1:])
        sent.append(after(value, same[1], same[chips - 1]))
        value = moved(sent[-1], [(0, through, far), (direct, direct, far)])
        halves = [jnp.where(section == s, value, half) for s, half in zip((through, direct), halves)]
    other = swapped(jnp.stack([same[r] for r in order]))
    dhidden = hidden_grad([after(same[0], *sent)] + [same[r] for r in order[1:]], other, w_down)
    near = [(f * chips + i, i, f) for f in range(2) for i in range(chips - 1)]
    near = local_gradients(dhidden, [arrived[r] for r in order[:-1]], near)
    last = local_gradients(dhidden, halves, [(f * chips + chips - 1, f, 0) for f in range(2)])
    hidden = [both[0][:, :, :skip]]
    hidden += [rotated(after(both[r][:, :, :skip], dhidden), r) for r in order[1:]]

    parts = 1
    width = mine.shape[1] // parts
    pieces, earlier = [], hidden[1:]
    for part in range(parts):
        kept, passed = terms(near, last, w_gate, w_up, chips, part * width, width)
        passed = swapped(after(passed, *earlier) if earlier else passed)
        sums = {r: summed(kept[i], passed[i]) for i, r in enumerate(order)}
        total, running = [relayed(sums[0], 0)], None
        if chips > 1:
            total.append(relayed(sums[chips - 1], chips - 1))
        earlier = total[:]
        for r in range(chips - 2, 0, -1):
            value = sums[r] if running is None else summed(sums[r], running)
            if r == 1:
                total.append(relayed(value, 1))
            else:
                running = rotated(value, -1)
                if len(earlier) < 3:
                    earlier.append(running)
        pieces.append(summed(*total))
    grad_input = jnp.concatenate(pieces, axis=1)

    block_grads = block_sums(
        after(own_columns(owner[0], cols[0], me), *sums.values()),
        [same[r] for r in order],
        other,
        hidden,
        1.0 / replicas,
    )
    return (grad_input[None], block_grads[None])


def solution(mesh):
    return jax.shard_map(
        shards,
        mesh=mesh,
        in_specs=(P("section", "dp", None),) * 6 + (P("section", None),) * 3,
        out_specs=(P("section", "dp", None), P("section", "dp", None, None)),
        check_vma=False,
    )
```

```python
import functools

import jax
import jax.numpy as jnp
from jax import lax
from jax.experimental import pallas as pl
from jax.experimental.pallas import tpu as pltpu
from jax.sharding import PartitionSpec as P

CAP = 3
LANES = 128
VMEM = 16 * 1024 * 1024
COST = pl.CostEstimate(flops=0, bytes_accessed=0, transcendentals=0)


def gelu(values):
    coeff = 0.7978845608
    tangent = jnp.tanh(coeff * (values + 0.044715 * (values * values * values)))
    return 0.5 * values * (1.0 + tangent)


def gelu_pair(values):
    coeff = 0.7978845608
    square = values * values
    tangent = jnp.tanh(coeff * (values + 0.044715 * (square * values)))
    activated = 0.5 * values * (1.0 + tangent)
    slope = 0.5 * (1.0 + tangent) + 0.5 * values * (1.0 - tangent * tangent) * coeff * (
        1.0 + 3.0 * 0.044715 * square
    )
    return activated, slope


def rotated(value, by):
    devices = lax.axis_size("dp")
    pairs = [(i, (i + 2 * by) % devices) for i in range(devices)]
    return lax.ppermute(value, "dp", pairs)


def swapped(value):
    return lax.ppermute(value, "dp", [(i, i ^ 1) for i in range(lax.axis_size("dp"))])


def moved(value, routes):
    devices = lax.axis_size("dp")
    pairs = [
        (first * devices + i, last * devices + (i + 2 * by) % devices)
        for first, last, by in routes
        for i in range(devices)
    ]
    return lax.ppermute(value, ("section", "dp"), pairs)


def relayed(value, by):
    return moved(value, [(s, s - 1, -by) for s in range(1, lax.axis_size("section"))])


def after(value, *earlier):
    return lax.optimization_barrier((value,) + earlier)[0]


def hidden_kernel(rows_ref, owner_ref, gate_ref, up_ref, out_ref, count_ref):
    out_ref[...] = jnp.zeros_like(out_ref)
    for replica in range(count_ref.shape[0]):
        count_ref[replica] = 0

    def block(i, carry):
        replica = owner_ref[i]
        slot = count_ref[replica]
        count_ref[replica] = slot + 1
        part = pl.ds(pl.multiple_of(rows_ref[i] * LANES, LANES), LANES)
        value = gelu(gate_ref[:, part].astype(jnp.float32)) * up_ref[:, part].astype(jnp.float32)
        place = pl.ds(pl.multiple_of((replica * CAP + slot) * LANES, LANES), LANES)
        out_ref[:, place] = value.astype(jnp.bfloat16)
        return carry

    lax.fori_loop(0, rows_ref.shape[0], block, 0)


def hidden_blocks(rows, owner, gate, up, replicas):
    tokens = gate.shape[0]
    return pl.pallas_call(
        hidden_kernel,
        in_specs=[pl.BlockSpec(memory_space=pltpu.SMEM)] * 2 + [pl.BlockSpec(memory_space=pltpu.VMEM)] * 2,
        out_specs=pl.BlockSpec(memory_space=pltpu.VMEM),
        out_shape=jax.ShapeDtypeStruct((tokens, replicas * CAP * LANES), jnp.bfloat16),
        scratch_shapes=[pltpu.SMEM((replicas,), jnp.int32)],
        compiler_params=pltpu.CompilerParams(vmem_limit_bytes=VMEM),
        cost_estimate=COST,
        name="hidden_blocks",
    )(rows, owner, gate, up)


def hidden_grad_kernel(*refs):
    same, (other_ref, w_ref, out_ref, sum_ref) = refs[:-4], refs[-4:]
    step = pl.program_id(0)
    value = lax.dot_general(
        jnp.concatenate([ref[...] for ref in same] + [other_ref[p] for p in range(len(same))], axis=0),
        w_ref[...],
        (((1,), (1,)), ((), ())),
        preferred_element_type=jnp.float32,
    )

    @pl.when(step == 0)
    def _():
        sum_ref[...] = value

    @pl.when(step > 0)
    def _():
        sum_ref[...] += value

    @pl.when(step == pl.num_programs(0) - 1)
    def _():
        out_ref[...] = sum_ref[...].astype(jnp.bfloat16)


def hidden_grad(same, other, weight):
    rows, width = same[0].shape
    units = weight.shape[0]
    tile = 8 * LANES
    out = (2 * len(same) * rows, units)
    return pl.pallas_call(
        hidden_grad_kernel,
        grid=(width // tile,),
        in_specs=[pl.BlockSpec((rows, tile), lambda i: (0, i))] * len(same)
        + [pl.BlockSpec((len(same), rows, tile), lambda i: (0, 0, i)), pl.BlockSpec((units, tile), lambda i: (0, i))],
        out_specs=pl.BlockSpec(out, lambda i: (0, 0)),
        out_shape=jax.ShapeDtypeStruct(out, jnp.bfloat16),
        scratch_shapes=[pltpu.VMEM(out, jnp.float32)],
        compiler_params=pltpu.CompilerParams(vmem_limit_bytes=VMEM),
        cost_estimate=COST,
        name="hidden_grad",
    )(*same, other, weight)


def gradients_kernel(blocks, dh_ref, *refs):
    given, out_ref = refs[:-1], refs[-1]
    units = dh_ref.shape[1]
    rows = given[0].shape[1]
    padded = given[0].shape[2] // 2
    for b, (block, i, f) in enumerate(blocks):
        part = slice(b * rows, (b + 1) * rows)
        wide = dh_ref[block * rows : (block + 1) * rows, :].astype(jnp.float32)
        gate = given[i][f, :, :units].astype(jnp.float32)
        up = given[i][f, :, padded : padded + units].astype(jnp.float32)
        activated, slope = gelu_pair(gate)
        out_ref[part, :units] = (wide * up * slope).astype(jnp.bfloat16)
        out_ref[part, units:] = (wide * activated).astype(jnp.bfloat16)


def local_gradients(dhidden, given, blocks):
    rows, units = len(blocks) * given[0].shape[1], dhidden.shape[1]
    return pl.pallas_call(
        functools.partial(gradients_kernel, blocks),
        in_specs=[pl.BlockSpec(memory_space=pltpu.VMEM)] * (1 + len(given)),
        out_specs=pl.BlockSpec(memory_space=pltpu.VMEM),
        out_shape=jax.ShapeDtypeStruct((rows, 2 * units), jnp.bfloat16),
        compiler_params=pltpu.CompilerParams(vmem_limit_bytes=VMEM),
        cost_estimate=COST,
        name="local_gradients",
    )(dhidden, *given)


def term_kernel(near_ref, far_ref, wg_ref, wu_ref, same_ref, other_ref):
    weight = jnp.concatenate([wg_ref[...], wu_ref[...]], axis=0)
    local = jnp.concatenate([near_ref[...], far_ref[...]], axis=0)
    term = jnp.dot(local, weight, preferred_element_type=jnp.float32).astype(jnp.bfloat16)
    chips, rows, tile = same_ref.shape
    near = near_ref.shape[0]
    for f, ref in enumerate((same_ref, other_ref)):
        ref[: chips - 1] = term[f * near // 2 : (f + 1) * near // 2].reshape(chips - 1, rows, tile)
        ref[chips - 1] = term[near + f * rows : near + (f + 1) * rows]


def terms(near, far, w_gate, w_up, chips, first, width):
    units = w_gate.shape[0]
    tile = 8 * LANES
    out = (chips, far.shape[0] // 2)
    return pl.pallas_call(
        term_kernel,
        grid=(width // tile,),
        in_specs=[pl.BlockSpec(near.shape, lambda i: (0, 0)), pl.BlockSpec(far.shape, lambda i: (0, 0))]
        + [pl.BlockSpec((units, tile), lambda i: (0, i + first // tile))] * 2,
        out_specs=[pl.BlockSpec(out + (tile,), lambda i: (0, 0, i))] * 2,
        out_shape=[jax.ShapeDtypeStruct(out + (width,), jnp.bfloat16)] * 2,
        compiler_params=pltpu.CompilerParams(vmem_limit_bytes=2 * VMEM),
        cost_estimate=COST,
        name="terms",
    )(near, far, w_gate, w_up)


def block_kernel(scale, cols_ref, other_ref, *refs):
    refs, out_ref = refs[:-1], refs[-1]
    same, hidden = refs[: len(refs) // 2], refs[len(refs) // 2 :]
    left = jnp.concatenate([ref[f] for f in range(2) for ref in hidden], axis=0)
    right = jnp.concatenate([ref[...] for ref in same] + [other_ref[p] for p in range(len(same))], axis=0)
    value = lax.dot_general(left, right, (((0,), (0,)), ((), ())), preferred_element_type=jnp.float32)
    out_ref[0] = (value * scale).astype(jnp.bfloat16)


def block_sums(cols, same, other, hidden, scale):
    rows = same[0].shape[0]
    return pl.pallas_call(
        functools.partial(block_kernel, scale),
        grid_spec=pltpu.PrefetchScalarGridSpec(
            num_scalar_prefetch=1,
            grid=(CAP,),
            in_specs=[pl.BlockSpec((len(same), rows, LANES), lambda k, cols_ref: (0, 0, cols_ref[k]))]
            + [pl.BlockSpec((rows, LANES), lambda k, cols_ref: (0, cols_ref[k]))] * len(same)
            + [pl.BlockSpec((2, rows, LANES), lambda k, cols_ref: (0, 0, k))] * len(hidden),
            out_specs=pl.BlockSpec((1, LANES, LANES), lambda k, cols_ref: (k, 0, 0)),
        ),
        out_shape=jax.ShapeDtypeStruct((CAP, LANES, LANES), jnp.bfloat16),
        compiler_params=pltpu.CompilerParams(vmem_limit_bytes=VMEM),
        cost_estimate=COST,
        name="block_sums",
    )(cols, other, *same, *hidden)


def summed(*values):
    total = values[0].astype(jnp.float32)
    for value in values[1:]:
        total = total + value.astype(jnp.float32)
    return total.astype(jnp.bfloat16)


def own_columns(rows_owner, cols, me):
    blocks = jnp.arange(cols.shape[0], dtype=jnp.int32)
    own = rows_owner == me
    earlier = own[None, :] & (blocks[None, :] < blocks[:, None])
    slots = jnp.sum(earlier.astype(jnp.int32), axis=1)
    hit = own[None, :] & (slots[None, :] == jnp.arange(CAP, dtype=jnp.int32)[:, None])
    return jnp.sum(jnp.where(hit, cols[None, :], 0), axis=1)


def shards(d_out, down_weight, gate_weight, up_weight, gate_pre, up_val, rows, cols, owner):
    mine = d_out[0]
    w_down, w_gate, w_up = down_weight[0], gate_weight[0], up_weight[0]
    gate, up = gate_pre[0], up_val[0]
    tokens = mine.shape[0]
    units = w_down.shape[0]
    replicas = lax.axis_size("dp")
    chips = replicas // 2
    me = lax.axis_index("dp")
    chip, core = me // 2, me % 2

    sections = lax.axis_size("section")
    section = lax.axis_index("section")

    same = [mine] + [None] * (chips - 1)
    same[1] = rotated(mine, 1)
    if chips > 2:
        same[chips - 1] = rotated(mine, -1)
    for r in range(chips - 2, 1, -1):
        same[r] = rotated(same[r + 1], -1)

    slots = hidden_blocks(rows[0], owner[0], gate, up, replicas)
    skip = CAP * LANES
    fill = jnp.zeros((tokens, -units % LANES), jnp.bfloat16)

    def held(replica):
        parts = [lax.dynamic_slice_in_dim(slots, replica * skip, skip, 1)]
        for values in (gate, up):
            parts += [lax.dynamic_slice_in_dim(values, replica * units, units, 1), fill]
        return jnp.concatenate(parts, axis=1)

    def ahead(r, other):
        return 2 * ((chip + r) % chips) + (1 - core if other else core)

    taken = swapped(jnp.stack([held(ahead(r, True)) for r in range(chips)]))
    both = [jnp.stack([held(ahead(r, False)), taken[r]]) for r in range(chips)]
    columns = [value[:, :, skip:] for value in both]

    far = chips // 2
    needed = range(1, sections)
    order = [r for r in range(chips) if r != far] + [far]
    passing = {s: moved(columns[far][:1], [(s, 0, 0)]) for s in needed}
    sent, arrived = [], {0: columns[0]}
    for r in order[1:]:
        if r != far:
            sent.append(after(columns[r], same[1], same[chips - 1]))
            arrived[r] = moved(sent[-1], [(s, s, r) for s in needed])
    halves = [jnp.zeros_like(passing[s]) for s in range(1, 3)]
    for k in range(sections - 1):
        through, direct = 1 + k, 1 + (k + 1) % (sections - 1)
        value = jnp.where(section == 0, passing[through], columns[far][1:])
        sent.append(after(value, same[1], same[chips - 1]))
        value = moved(sent[-1], [(0, through, far), (direct, direct, far)])
        halves = [jnp.where(section == s, value, half) for s, half in zip((through, direct), halves)]
    other = swapped(jnp.stack([same[r] for r in order]))
    dhidden = hidden_grad([after(same[0], *sent)] + [same[r] for r in order[1:]], other, w_down)
    near = [(f * chips + i, i, f) for f in range(2) for i in range(chips - 1)]
    near = local_gradients(dhidden, [arrived[r] for r in order[:-1]], near)
    last = local_gradients(dhidden, halves, [(f * chips + chips - 1, f, 0) for f in range(2)])
    hidden = [both[0][:, :, :skip]]
    hidden += [rotated(after(both[r][:, :, :skip], dhidden), r) for r in order[1:]]

    parts = 1
    width = mine.shape[1] // parts
    pieces, earlier = [], hidden[1:]
    for part in range(parts):
        kept, passed = terms(near, last, w_gate, w_up, chips, part * width, width)
        passed = swapped(after(passed, *earlier) if earlier else passed)
        sums = {r: summed(kept[i], passed[i]) for i, r in enumerate(order)}
        total, running = [relayed(sums[0], 0)], None
        if chips > 1:
            total.append(relayed(sums[chips - 1], chips - 1))
        earlier = total[:]
        for r in range(chips - 2, 0, -1):
            value = sums[r] if running is None else summed(sums[r], running)
            if r == 1:
                total.append(relayed(value, 1))
            else:
                running = rotated(value, -1)
                if len(earlier) < 3:
                    earlier.append(running)
        pieces.append(summed(*total))
    grad_input = jnp.concatenate(pieces, axis=1)

    block_grads = block_sums(
        after(own_columns(owner[0], cols[0], me), *sums.values()),
        [same[r] for r in order],
        other,
        hidden,
        1.0 / replicas,
    )
    return (grad_input[None], block_grads[None])


def solution(mesh):
    return jax.shard_map(
        shards,
        mesh=mesh,
        in_specs=(P("section", "dp", None),) * 6 + (P("section", None),) * 3,
        out_specs=(P("section", "dp", None), P("section", "dp", None, None)),
        check_vma=False,
    )
```
